256 devices in a mesh: rcv: 8 (over y, core), src: 32 (over z, x).
Axes of the slice: x: 4, y: 4, z: 8, core: 2. Of those that a mesh axis runs over, the one named last changes fastest.
Arguments:
- kernel: float32 [24576, 24576], P('rcv', 'src'), may hold values from -0.078125 to 0.078125
- self_stiffness: float32 [24576], P(('rcv', 'src')), may hold values from 0.5 to 2
- slip: float32 [24576, 128], P(('rcv', 'src')), may hold values from -6 to 6
- state: float32 [24576, 128], P(('rcv', 'src')), may hold values from -0.5 to 0.5
- stress: float32 [24576, 128], P(('rcv', 'src')), may hold values from -0.5 to 0.5
- section_id: int32 [24576], P(('rcv', 'src')), may hold values from 0 to 15, never falling along the last dimension, each value on 1 to 3072 neighbouring positions
- scenario_param: int32 [128], replicated, may hold values from 0 to 7
- direct_table: float32 [16], replicated, may hold values from 0.6 to 1.2
- evolve_table: float32 [16], replicated, may hold values from 0.3 to 0.8
- load_table: float32 [8, 16], replicated, may hold values from 0.3 to 1.5
Outputs:
- slip_new: float32 [24576, 128], P(('rcv', 'src'))
- state_new: float32 [24576, 128], P(('rcv', 'src'))
- stress_new: float32 [24576, 128], P(('rcv', 'src'))
The draws below stay inside these ranges and needn't reach their ends.
Inputs may be any that keep to these rules, and one draw needn't show every extreme that they name: `section_id`: each section is one contiguous run of patches, in rising order.
All inputs are finite; a program needn't handle non-finite values.
Results may differ from the reference program's by a relative error of at most 0.0001.
Values sent between devices are 32-bit elements; how exact they have to be, the bound alone decides.
No kernel may reach another device: no remote copies, remote signals or barrier semaphores. Data moves between devices by JAX's collectives and lax.ppermute only.
A program may use at most 64 MiB of HBM per device.

```python
import math
import jax
import jax.numpy as jnp
import numpy as np
from jax import lax

P_SIZE = 24576
S = 128
NSEC = 16
NPAR = 8


def plant(result, rng, low, top_value):
    shape = result.shape
    index_at = [jax.random.randint(jax.random.fold_in(rng, axis), (), 0, shape[axis]) for axis in range(len(shape))]
    result = result.at[tuple(index_at)].set(low)
    longest = shape.index(max(shape))
    index_at[longest] = (index_at[longest] + 1) % shape[longest]
    return result.at[tuple(index_at)].set(top_value)


def strengthened(drawn, own_key, source, target, shards_of, factor):
    owner, partner = [(jnp.arange(drawn.shape[position]) // (drawn.shape[position] // shards_of)).reshape([-1 if axis == position else 1 for axis in range(drawn.ndim)]) for position in (source, target)]
    chosen = jax.random.permutation(own_key, shards_of)[partner]
    strong = (owner == chosen) | (owner == (partner + shards_of // 2) % shards_of)
    return jnp.where(strong, factor * drawn, drawn)


def block_levels(stream_key, extent, cuts, low, top_value):
    loudness, own = 1.0, jax.random.fold_in(stream_key, 6)
    for dim, shards_of in cuts:
        draws = jnp.exp(jax.random.uniform(jax.random.fold_in(own, dim), (shards_of,), jnp.float32, low / len(cuts), top_value / len(cuts)))
        loudness = loudness * jnp.repeat(draws, extent[dim] // shards_of).reshape([-1 if axis == dim else 1 for axis in range(len(extent))])
    return loudness


def length_profile(count, total, most, skew):
    weights = [(1 << 20) // math.isqrt(grade ** skew) + 1 for grade in range(2, count + 1)]
    spare, holding = total - most - (count - 1), [1] * (count - 1)
    while spare > 0:
        movable = [i for i in range(count - 1) if holding[i] < most]
        pool, left = sum([weights[i] for i in movable]), spare
        for i in movable:
            extra = min(most - holding[i], max(1, left * weights[i] // pool), spare)
            holding[i] = holding[i] + extra
            spare = spare - extra
    return np.array([most] + holding)


def ragged_sizes(own_key, amount, total, most, slope):
    if amount == 2:
        one = jax.random.randint(own_key, (), max(1, total - most), min(most, total - 1) + 1)
        return jnp.stack([one, total - one])
    lengths = jnp.asarray(length_profile(amount, total, most, slope), jnp.int32)
    twos = (amount - 1) // 2
    source_of, receiver = lengths[1:1 + 2 * twos:2], lengths[2:2 + 2 * twos:2]
    margin = jnp.minimum(source_of - 1, most - receiver)
    moved = jax.random.randint(jax.random.fold_in(own_key, 1), (twos,), 0, 1 << 20) % (margin + 1)
    lengths = lengths.at[1:1 + 2 * twos:2].set(source_of - moved).at[2:2 + 2 * twos:2].set(receiver + moved)
    return lengths[jax.random.permutation(jax.random.fold_in(own_key, 2), amount)]


def bell_draw(key, extent, spread, limit, pieces=(), kind=jnp.bfloat16):
    drawn = jax.random.normal(key, extent, jnp.float32) * spread
    if len(pieces) > 0:
        drawn = block_levels(key, extent, pieces, -0.22, 0.18) * drawn
    return jnp.clip(drawn, min=-limit, max=limit).astype(kind)


def noise_with(key, dims, spread, reach, pieces, heavy, held_as=jnp.bfloat16):
    entries = spread * jax.random.normal(key, dims, jnp.float32)
    if pieces:
        entries = entries * block_levels(key, dims, pieces, -0.22, 0.18)
    return jnp.clip(strengthened(entries, jax.random.fold_in(key, 3), *heavy), -reach, reach).astype(held_as)


def setup_inputs(seed: int = 0) -> dict:
    keys = jax.random.split(jax.random.key(seed), 11)
    return {
        "kernel": noise_with(keys[0], (P_SIZE, P_SIZE), P_SIZE ** -0.5, 0.078125, ((0, 8), (1, 32)), (1, 0, 32, 2.75), jnp.float32),
        "self_stiffness": jnp.clip(jnp.exp(math.log(2.0) - 1.3862944 * jax.random.uniform(keys[1], (P_SIZE,), jnp.float32) ** block_levels(keys[1], (P_SIZE,), ((0, 256),), -0.2, 0.2)), 0.5, 2.0),
        "slip": bell_draw(keys[2], (P_SIZE, S), 1.0, 6.0, ((0, 256),), jnp.float32),
        "state": jnp.clip(jax.random.uniform(keys[3], (P_SIZE, S), jnp.float32, -0.5, 0.5) * block_levels(keys[3], (P_SIZE, S), ((0, 256),), -0.4, 0.0), -0.5, 0.5),
        "stress": jnp.clip(jax.random.uniform(keys[4], (P_SIZE, S), jnp.float32, -0.5, 0.5) * block_levels(keys[4], (P_SIZE, S), ((0, 256),), -0.4, 0.0), -0.5, 0.5),
        "section_id": jnp.searchsorted(jnp.cumsum(ragged_sizes(keys[5], NSEC, P_SIZE, P_SIZE // 8, 2)), jnp.arange(P_SIZE), side="right").astype(jnp.int32),
        "scenario_param": plant(jax.random.randint(keys[6], (S,), 0, NPAR), jax.random.fold_in(keys[6], 1), 0, NPAR - 1).astype(jnp.int32),
        "direct_table": jnp.clip(jnp.exp(jax.random.uniform(keys[7], (NSEC,), jnp.float32, math.log(0.6), math.log(1.2))), 0.6, 1.2),
        "evolve_table": jnp.clip(jax.random.uniform(keys[8], (NSEC,), jnp.float32, 0.3, 0.8), 0.3, 0.8),
        "load_table": jnp.clip(jnp.exp(jax.random.uniform(keys[9], (NPAR, NSEC), jnp.float32, math.log(0.3), math.log(1.5))), 0.3, 1.5),
    }


step_size = 0.1


def lookups(section_id, scenario_param, direct_table, evolve_table, load_table):
    sections = direct_table.shape[0]
    settings = load_table.shape[0]
    section_onehot = (section_id[:, None] == jnp.arange(sections, dtype=jnp.int32)[None, :]).astype(jnp.float32)
    setting_onehot = (scenario_param[:, None] == jnp.arange(settings, dtype=jnp.int32)[None, :]).astype(jnp.float32)
    direct = jnp.dot(section_onehot, direct_table, precision=lax.Precision.HIGHEST)
    evolve = jnp.dot(section_onehot, evolve_table, precision=lax.Precision.HIGHEST)
    load_pick = jnp.dot(setting_onehot, load_table, precision=lax.Precision.HIGHEST)
    plate = jnp.dot(section_onehot, load_pick.T, precision=lax.Precision.HIGHEST)
    return direct, evolve, plate


def reference(kernel, self_stiffness, slip, state, stress, section_id, scenario_param, direct_table, evolve_table, load_table):
    direct, evolve, plate = lookups(section_id, scenario_param, direct_table, evolve_table, load_table)

    def derivative(state_now, stress_now):
        slip_rate = jnp.exp((stress_now - evolve[:, None] * state_now) / direct[:, None])
        mismatch = slip_rate - plate
        coupled = jnp.dot(kernel, mismatch, precision=lax.Precision.HIGHEST, preferred_element_type=jnp.float32)
        stress_rate = -self_stiffness[:, None] * mismatch - coupled
        state_rate = jnp.exp(-state_now) - slip_rate
        return slip_rate, state_rate, stress_rate

    weights = (1.0, 2.0, 2.0, 1.0)
    offsets = (0.0, 0.5, 0.5, 1.0)
    sum_slip = jnp.zeros_like(slip)
    sum_state = jnp.zeros_like(state)
    sum_stress = jnp.zeros_like(stress)
    last = None
    for phase_index in range(4):
        if phase_index == 0:
            state_now, stress_now = state, stress
        else:
            state_now = state + offsets[phase_index] * step_size * last[1]
            stress_now = stress + offsets[phase_index] * step_size * last[2]
        last = derivative(state_now, stress_now)
        sum_slip = sum_slip + weights[phase_index] * last[0]
        sum_state = sum_state + weights[phase_index] * last[1]
        sum_stress = sum_stress + weights[phase_index] * last[2]
    slip_new = slip + (step_size / 6.0) * sum_slip
    state_new = state + (step_size / 6.0) * sum_state
    stress_new = stress + (step_size / 6.0) * sum_stress
    return slip_new, state_new, stress_new
```

```python
import jax
import jax.numpy as jnp
import numpy as np
from jax import lax
from jax.experimental import pallas as pl
from jax.experimental.pallas import tpu as pltpu
from jax.sharding import Mesh
from jax.sharding import PartitionSpec as P

step_size = 0.1
AXES = ("y", "core", "zp", "zl", "x")
SIZES = (4, 2, 4, 2, 4)
SHARD = 96
HALF = 4 * SHARD


def index_of(place):
    index = 0
    for coordinate, size in zip(place, SIZES):
        index = index * size + coordinate
    return index


def moved(array, target):
    places = np.ndindex(*SIZES)
    return lax.ppermute(array, AXES, [(index_of(p), index_of(target(*p))) for p in places])


def rotated(array, axis, distance):
    size = SIZES[AXES.index(axis)]
    return lax.ppermute(array, axis, [(i, (i + distance) % size) for i in range(size)])


def to_worker(y, c, zp, zl, x):
    return (x, zl, y, c, zp)


def to_owner(y, c, zp, zl, x):
    return (zp, zl, x, c, y)


def crossed(y, c, zp, zl, x):
    return (zp, zl, y, c, x)


def product_kernel(core_ref, tile_ref, own_ref, other_ref, out_ref, columns):
    @pl.when(pl.program_id(0) == 0)
    def _():
        core = core_ref[0]
        for part, half in ((own_ref, core), (other_ref, 1 - core)):
            value = part[...]
            high = value.astype(jnp.bfloat16)
            rows = pl.ds(pl.multiple_of(half * HALF, HALF), HALF)
            columns[rows, :128] = high
            columns[rows, 128:] = (value - high.astype(jnp.float32)).astype(jnp.bfloat16)

    tile = tile_ref[...]
    high = tile.astype(jnp.bfloat16)
    low = (tile - high.astype(jnp.float32)).astype(jnp.bfloat16)
    main = jnp.dot(high, columns[...], preferred_element_type=jnp.float32)
    rest = jnp.dot(low, columns[:, :128], preferred_element_type=jnp.float32)
    total = main[:, :128] + (main[:, 128:] + rest)
    out_ref[...] = total.reshape(out_ref.shape)


def product(core, kernel, own, other, last):
    if last:
        out_spec = pl.BlockSpec((1, 4, 1, SHARD, 128), lambda d, core: (d // 4, 0, d % 4, 0, 0))
    else:
        out_spec = pl.BlockSpec((1, 1, 4, SHARD, 128), lambda d, core: (d // 4, d % 4, 0, 0, 0))
    return pl.pallas_call(
        product_kernel,
        grid_spec=pltpu.PrefetchScalarGridSpec(
            num_scalar_prefetch=1,
            grid=(8,),
            in_specs=[
                pl.BlockSpec((HALF, 768), lambda d, core: (d % 4 * 2 + d // 4, 0)),
                pl.BlockSpec((HALF, 128), lambda d, core: (0, 0)),
                pl.BlockSpec((HALF, 128), lambda d, core: (0, 0)),
            ],
            out_specs=out_spec,
            scratch_shapes=[pltpu.VMEM((768, 256), jnp.bfloat16)],
        ),
        out_shape=jax.ShapeDtypeStruct((2, 4, 4, SHARD, 128), jnp.float32),
        compiler_params=pltpu.CompilerParams(vmem_limit_bytes=24 * 1024 * 1024),
        cost_estimate=pl.CostEstimate(
            flops=2 * 3072 * 768 * 512, bytes_accessed=12 * 1024 * 1024, transcendentals=0
        ),
    )(core, kernel, own, other)


def lookups(section_id, scenario_param, direct_table, evolve_table, load_table):
    sections = direct_table.shape[0]
    settings = load_table.shape[0]
    section_onehot = (section_id[:, None] == jnp.arange(sections, dtype=jnp.int32)[None, :]).astype(
        jnp.float32
    )
    setting_onehot = (
        scenario_param[:, None] == jnp.arange(settings, dtype=jnp.int32)[None, :]
    ).astype(jnp.float32)
    direct = jnp.dot(section_onehot, direct_table, precision=lax.Precision.HIGHEST)
    evolve = jnp.dot(section_onehot, evolve_table, precision=lax.Precision.HIGHEST)
    load_pick = jnp.dot(setting_onehot, load_table, precision=lax.Precision.HIGHEST)
    plate = jnp.dot(section_onehot, load_pick.T, precision=lax.Precision.HIGHEST)
    return (direct, evolve, plate)


def gathered_over_y(array):
    rows = array.shape[0]
    parts = [rotated(array, "y", t) for t in (2, 1, 3)]
    second, first, third = parts
    ring = jnp.concatenate([third, second, first, array, third, second, first])
    start = (3 - lax.axis_index("y")) * rows
    return lax.dynamic_slice_in_dim(ring, start, 4 * rows, 0).reshape(4, rows, 128)


def local(
    kernel,
    self_stiffness,
    slip,
    state,
    stress,
    section_id,
    scenario_param,
    direct_table,
    evolve_table,
    load_table,
):
    core = lax.axis_index("core").astype(jnp.int32).reshape(1)
    scalars = jnp.pad(
        jnp.stack([section_id.astype(jnp.float32), self_stiffness]), ((0, 6), (0, 128 - SHARD))
    )
    sent = moved(jnp.concatenate([state, stress, scalars]), to_worker)
    here = gathered_over_y(sent)
    state_0 = here[:, :SHARD].reshape(HALF, 128)
    stress_0 = here[:, SHARD : 2 * SHARD].reshape(HALF, 128)
    sections = here[:, 2 * SHARD, :SHARD].reshape(HALF).astype(jnp.int32)
    stiffness = here[:, 2 * SHARD + 1, :SHARD].reshape(HALF)[:, None]
    direct, evolve, plate = lookups(
        sections, scenario_param, direct_table, evolve_table, load_table
    )
    direct, evolve = direct[:, None], evolve[:, None]

    weights = (1.0, 2.0, 2.0, 1.0)
    offsets = (0.0, 0.5, 0.5, 1.0)
    sum_slip = sum_state = sum_stress = 0.0
    state_rate = stress_rate = None
    for phase in range(4):
        if phase == 0:
            state_now, stress_now = (state_0, stress_0)
        else:
            state_now = state_0 + offsets[phase] * step_size * state_rate
            stress_now = stress_0 + offsets[phase] * step_size * stress_rate
        slip_rate = jnp.exp((stress_now - evolve * state_now) / direct)
        mismatch = slip_rate - plate
        other = rotated(mismatch, "core", 1)
        partial = product(core, kernel, mismatch, other, phase == 3)
        state_rate = jnp.exp(-state_now) - slip_rate
        sum_slip = sum_slip + weights[phase] * slip_rate
        sum_state = sum_state + weights[phase] * state_rate
        own_rate = -stiffness * mismatch
        if phase == 3:
            break
        spread = lax.all_to_all(partial.reshape(8, HALF, 128), ("zl", "x"), 0, 0)
        across = moved(spread.sum(0), crossed)
        coupled = across
        for distance in (2, 1, 3):
            coupled = coupled + rotated(across, "y", distance)
        stress_rate = own_rate - coupled
        sum_stress = sum_stress + weights[phase] * stress_rate
    sums = jnp.stack([sum_slip, sum_state, sum_stress + own_rate]).reshape(3, 4, SHARD, 128)
    mine = lax.dynamic_index_in_dim(sums, lax.axis_index("y"), 1, keepdims=False)
    back = moved(mine, to_owner)
    spread = lax.all_to_all(partial.reshape(8, HALF, 128), ("zl", "x"), 0, 0).sum(0)
    coupled = lax.all_to_all(spread.reshape(4, SHARD, 128), "zp", 0, 0).sum(0)
    slip_new = slip + step_size / 6.0 * back[0]
    state_new = state + step_size / 6.0 * back[1]
    stress_new = stress + step_size / 6.0 * (back[2] - coupled)
    return (slip_new, state_new, stress_new)


def solution(mesh):
    fine = Mesh(np.asarray(mesh.devices).reshape(SIZES), AXES)
    in_specs = (
        P(("y", "core"), ("zp", "zl", "x")),
        P(AXES),
        P(AXES, None),
        P(AXES, None),
        P(AXES, None),
        P(AXES),
        P(),
        P(),
        P(),
        P(),
    )
    out_specs = (P(AXES, None), P(AXES, None), P(AXES, None))
    return jax.shard_map(local, mesh=fine, in_specs=in_specs, out_specs=out_specs, check_vma=False)
```

```python
import jax
import jax.numpy as jnp
import numpy as np
from jax import lax
from jax.experimental import pallas as pl
from jax.experimental.pallas import tpu as pltpu
from jax.sharding import Mesh
from jax.sharding import PartitionSpec as P

step_size = 0.1
AXES = ("y", "core", "zp", "zl", "x")
SIZES = (4, 2, 4, 2, 4)
SHARD = 96
HALF = 4 * SHARD
SPREAD = (((2, 1), (2, 0)), ((1, 1), (3, 1), (1, 0), (3, 0)), ((0, 1), (0, 0)))


def index_of(place):
    index = 0
    for coordinate, size in zip(place, SIZES):
        index = index * size + coordinate
    return index


def moved(array, target):
    places = np.ndindex(*SIZES)
    return lax.ppermute(array, AXES, [(index_of(p), index_of(target(*p))) for p in places])


def rotated(array, axis, distance):
    size = SIZES[AXES.index(axis)]
    return lax.ppermute(array, axis, [(i, (i + distance) % size) for i in range(size)])


def to_worker(y, c, zp, zl, x):
    return (x, zl, y, c, zp)


def to_owner(y, c, zp, zl, x):
    return (zp, zl, x, c, y)


def split(value):
    high = value.astype(jnp.bfloat16)
    return high, (value - high.astype(jnp.float32)).astype(jnp.bfloat16)


def split_kernel(tile_ref, out_ref):
    half = pl.program_id(0)
    high, low = split(tile_ref[...])
    out_ref[half // 2, half % 2, :, 0] = high.reshape(4, SHARD, 768)
    out_ref[half // 2, half % 2, :, 1] = low.reshape(4, SHARD, 768)


def split_tile(kernel):
    shape = (4, 2, 4, 2, SHARD, 768)
    return pl.pallas_call(
        split_kernel,
        grid=(8,),
        in_specs=[pl.BlockSpec((HALF, 768), lambda d: (d, 0))],
        out_specs=pl.BlockSpec(memory_space=pltpu.VMEM),
        out_shape=pltpu.VMEM(shape, jnp.bfloat16),
        compiler_params=pltpu.CompilerParams(vmem_limit_bytes=52 * 1024 * 1024),
        cost_estimate=pl.CostEstimate(
            flops=4 * 3072 * 768, bytes_accessed=3072 * 768 * 8, transcendentals=0
        ),
    )(kernel)


def product_kernel(steps, last, first, *refs):
    place_ref, tile_ref = refs[:2]
    y, core, zp, zl, x = [place_ref[i] for i in range(5)]
    if first:
        own_ref, other_ref, columns_ref = refs[2], refs[3], refs[-1]
        outs = refs[4:-1]
        for half_ref, half in ((own_ref, core), (other_ref, 1 - core)):
            for t in range(4):
                high, low = split(half_ref[t * SHARD : (t + 1) * SHARD])
                start = half * HALF + lax.rem(y + 4 - t, 4) * SHARD
                rows = pl.ds(pl.multiple_of(start, SHARD), SHARD)
                columns_ref[rows, :128] = high
                columns_ref[rows, 128:] = low
    else:
        columns_ref, outs = refs[2], refs[3:]
    columns = columns_ref[...]
    for (dx, dz), out_ref in zip(steps, outs):
        there = lax.rem(x + dx, 4)
        half = lax.rem(zl + dz, 2)
        if last:
            tile = tile_ref[:, half, there]
        else:
            tile = tile_ref[there, half]
        sums = jnp.dot(
            tile.reshape(2 * HALF, 768), columns, preferred_element_type=jnp.float32
        ).reshape(4, 2, SHARD, 256)
        total = sums[:, 0, :, :128] + (sums[:, 0, :, 128:] + sums[:, 1, :, :128])
        for i in range(4):
            start = lax.rem(i + 4 - zp, 4) * SHARD
            out_ref[pl.ds(pl.multiple_of(start, SHARD), SHARD)] = total[i]


def product(place, tile, own, other, last):
    result = {}
    columns = None
    block = jax.ShapeDtypeStruct((HALF, 128), jnp.float32)
    on_chip = pl.BlockSpec(memory_space=pltpu.VMEM)
    for steps in SPREAD:
        first = columns is None
        given = (own, other) if first else (columns,)
        out_shape = [block] * len(steps)
        if first:
            out_shape.append(jax.ShapeDtypeStruct((768, 256), jnp.bfloat16))

        def body(*refs, steps=steps, first=first):
            product_kernel(steps, last, first, *refs)

        outs = pl.pallas_call(
            body,
            in_specs=[pl.BlockSpec(memory_space=pltpu.SMEM)] + [on_chip] * (1 + len(given)),
            out_specs=[on_chip] * len(out_shape),
            out_shape=out_shape,
            compiler_params=pltpu.CompilerParams(vmem_limit_bytes=16 * 1024 * 1024),
            cost_estimate=pl.CostEstimate(
                flops=len(steps) * 2 * 768 * 768 * 256, bytes_accessed=2 * 1024 * 1024, transcendentals=0
            ),
        )(place, tile, *given)
        if first:
            columns = outs[-1]
        result.update(zip(steps, outs))
    return result


def lookups(section_id, scenario_param, direct_table, evolve_table, load_table):
    sections = direct_table.shape[0]
    settings = load_table.shape[0]
    section_onehot = (section_id[:, None] == jnp.arange(sections, dtype=jnp.int32)[None, :]).astype(
        jnp.float32
    )
    setting_onehot = (
        scenario_param[:, None] == jnp.arange(settings, dtype=jnp.int32)[None, :]
    ).astype(jnp.float32)
    direct = jnp.dot(section_onehot, direct_table, precision=lax.Precision.HIGHEST)
    evolve = jnp.dot(section_onehot, evolve_table, precision=lax.Precision.HIGHEST)
    load_pick = jnp.dot(setting_onehot, load_table, precision=lax.Precision.HIGHEST)
    plate = jnp.dot(section_onehot, load_pick.T, precision=lax.Precision.HIGHEST)
    return (direct, evolve, plate)


def summed_over_zl_and_x(partial):
    total = partial[0, 0]
    for steps in SPREAD:
        for dx, dz in steps:
            if (dx, dz) != (0, 0):
                total = total + moved(
                    partial[dx, dz],
                    lambda y, c, zp, zl, x: (y, c, zp, (zl + dz) % 2, (x + dx) % 4),
                )
    return total


def summed_over_zp(blocks):
    total = 0.0
    for p in (2, 1, 3, 0):
        total = total + moved(
            blocks[p * SHARD : (p + 1) * SHARD],
            lambda y, c, zp, zl, x: ((p + zp) % 4, zl, y, c, x),
        )
    return total


def local(
    kernel,
    self_stiffness,
    slip,
    state,
    stress,
    section_id,
    scenario_param,
    direct_table,
    evolve_table,
    load_table,
):
    place = jnp.stack([lax.axis_index(axis).astype(jnp.int32) for axis in AXES])
    tile = split_tile(kernel)
    scalars = jnp.pad(
        jnp.stack([section_id.astype(jnp.float32), self_stiffness]), ((0, 6), (0, 128 - SHARD))
    )
    here = moved(jnp.concatenate([state, stress, scalars]), to_worker)
    here, tile = lax.optimization_barrier((here, tile))
    state_0 = here[:SHARD]
    stress_0 = here[SHARD : 2 * SHARD]
    sections = here[2 * SHARD, :SHARD].astype(jnp.int32)
    stiffness = here[2 * SHARD + 1, :SHARD][:, None]
    direct, evolve, plate = lookups(
        sections, scenario_param, direct_table, evolve_table, load_table
    )
    direct, evolve = direct[:, None], evolve[:, None]

    weights = (1.0, 2.0, 2.0, 1.0)
    offsets = (0.0, 0.5, 0.5, 1.0)
    sum_slip = sum_state = sum_stress = 0.0
    state_rate = stress_rate = None
    for phase in range(4):
        if phase == 0:
            state_now, stress_now = (state_0, stress_0)
        else:
            state_now = state_0 + offsets[phase] * step_size * state_rate
            stress_now = stress_0 + offsets[phase] * step_size * stress_rate
        slip_rate = jnp.exp((stress_now - evolve * state_now) / direct)
        mismatch = slip_rate - plate
        along_y = [mismatch] + [rotated(mismatch, "y", t) for t in (1, 2, 3)]
        own = jnp.concatenate(along_y)
        partial = product(place, tile, own, rotated(own, "core", 1), phase == 3)
        state_rate = jnp.exp(-state_now) - slip_rate
        sum_slip = sum_slip + weights[phase] * slip_rate
        sum_state = sum_state + weights[phase] * state_rate
        own_rate = -stiffness * mismatch
        blocks = summed_over_zl_and_x(partial)
        if phase == 3:
            break
        stress_rate = own_rate - summed_over_zp(blocks)
        sum_stress = sum_stress + weights[phase] * stress_rate
    back = moved(jnp.concatenate([sum_slip, sum_state, sum_stress + own_rate]), to_owner)
    coupled = blocks[:SHARD]
    for p in (2, 1, 3):
        coupled = coupled + rotated(blocks[p * SHARD : (p + 1) * SHARD], "zp", p)
    slip_new = slip + step_size / 6.0 * back[:SHARD]
    state_new = state + step_size / 6.0 * back[SHARD : 2 * SHARD]
    stress_new = stress + step_size / 6.0 * (back[2 * SHARD :] - coupled)
    return (slip_new, state_new, stress_new)


def solution(mesh):
    fine = Mesh(np.asarray(mesh.devices).reshape(SIZES), AXES)
    in_specs = (
        P(("y", "core"), ("zp", "zl", "x")),
        P(AXES),
        P(AXES, None),
        P(AXES, None),
        P(AXES, None),
        P(AXES),
        P(),
        P(),
        P(),
        P(),
    )
    out_specs = (P(AXES, None), P(AXES, None), P(AXES, None))
    return jax.shard_map(local, mesh=fine, in_specs=in_specs, out_specs=out_specs, check_vma=False)
```

```python
import jax
import jax.numpy as jnp
import numpy as np
from jax import lax
from jax.experimental import pallas as pl
from jax.experimental.pallas import tpu as pltpu
from jax.sharding import Mesh
from jax.sharding import PartitionSpec as P

step_size = 0.1
AXES = ("y", "core", "zp", "zl", "x")
SIZES = (4, 2, 4, 2, 4)
SHARD = 96
HALF = 4 * SHARD
SPREAD = (((2, 1), (1, 1), (3, 1)), ((0, 1), (2, 0), (1, 0), (3, 0), (0, 0)))


def index_of(place):
    index = 0
    for coordinate, size in zip(place, SIZES):
        index = index * size + coordinate
    return index


def moved(array, target):
    places = np.ndindex(*SIZES)
    return lax.ppermute(array, AXES, [(index_of(p), index_of(target(*p))) for p in places])


def rotated(array, axis, distance):
    size = SIZES[AXES.index(axis)]
    return lax.ppermute(array, axis, [(i, (i + distance) % size) for i in range(size)])


def to_worker(y, c, zp, zl, x):
    return (x, zl, y, c, zp)


def to_owner(y, c, zp, zl, x):
    return (zp, zl, x, c, y)


def split(value):
    high = value.astype(jnp.bfloat16)
    return high, (value - high.astype(jnp.float32)).astype(jnp.bfloat16)


def split_kernel(tile_ref, out_ref, token_ref):
    half = pl.program_id(0)
    token_ref[...] = jnp.zeros((8, 128), jnp.float32)
    high, low = split(tile_ref[...])
    out_ref[half // 2, half % 2, :, 0] = high.reshape(4, SHARD, 768)
    out_ref[half // 2, half % 2, :, 1] = low.reshape(4, SHARD, 768)


def split_tile(kernel):
    shape = (4, 2, 4, 2, SHARD, 768)
    return pl.pallas_call(
        split_kernel,
        grid=(8,),
        in_specs=[pl.BlockSpec((HALF, 768), lambda d: (d, 0))],
        out_specs=[pl.BlockSpec(memory_space=pltpu.VMEM), pl.BlockSpec((8, 128), lambda d: (0, 0))],
        out_shape=[pltpu.VMEM(shape, jnp.bfloat16), jax.ShapeDtypeStruct((8, 128), jnp.float32)],
        compiler_params=pltpu.CompilerParams(vmem_limit_bytes=20 * 1024 * 1024),
        cost_estimate=pl.CostEstimate(
            flops=4 * 3072 * 768, bytes_accessed=3072 * 768 * 8, transcendentals=0
        ),
    )(kernel)


def product_kernel(steps, last, first, *refs):
    place_ref, tile_ref, _, *refs = refs
    y, core, zp, zl, x = [place_ref[i] for i in range(5)]
    if first:
        own_ref, other_ref, columns_ref = refs[0], refs[1], refs[-1]
        outs = refs[2:-1]
        for half_ref, half in ((own_ref, core), (other_ref, 1 - core)):
            for t in range(4):
                high, low = split(half_ref[t * SHARD : (t + 1) * SHARD])
                start = half * HALF + lax.rem(y + 4 - t, 4) * SHARD
                rows = pl.ds(pl.multiple_of(start, SHARD), SHARD)
                columns_ref[rows, :128] = high
                columns_ref[rows, 128:] = low
    else:
        columns_ref, outs = refs[0], refs[1:]
    columns = columns_ref[...]
    for (dx, dz), out_ref in zip(steps, outs):
        there = lax.rem(x + dx, 4)
        half = lax.rem(zl + dz, 2)
        if last:
            tile = tile_ref[:, half, there]
        else:
            tile = tile_ref[there, half]
        sums = jnp.dot(
            tile.reshape(2 * HALF, 768), columns, preferred_element_type=jnp.float32
        ).reshape(4, 2, SHARD, 256)
        total = sums[:, 0, :, :128] + (sums[:, 0, :, 128:] + sums[:, 1, :, :128])
        for i in range(4):
            start = lax.rem(i + 4 - zp, 4) * SHARD
            out_ref[pl.ds(pl.multiple_of(start, SHARD), SHARD)] = total[i]


def product(place, tile, token, own, other, last):
    result = {}
    columns = None
    block = jax.ShapeDtypeStruct((HALF, 128), jnp.float32)
    on_chip = pl.BlockSpec(memory_space=pltpu.VMEM)
    for steps in SPREAD:
        first = columns is None
        given = (own, other) if first else (columns,)
        out_shape = [block] * len(steps)
        if first:
            out_shape.append(jax.ShapeDtypeStruct((768, 256), jnp.bfloat16))

        def body(*refs, steps=steps, first=first):
            product_kernel(steps, last, first, *refs)

        outs = pl.pallas_call(
            body,
            in_specs=[pl.BlockSpec(memory_space=pltpu.SMEM)] + [on_chip] * (2 + len(given)),
            out_specs=[on_chip] * len(out_shape),
            out_shape=out_shape,
            compiler_params=pltpu.CompilerParams(vmem_limit_bytes=16 * 1024 * 1024),
            cost_estimate=pl.CostEstimate(
                flops=len(steps) * 2 * 768 * 768 * 256, bytes_accessed=2 * 1024 * 1024, transcendentals=0
            ),
        )(place, tile, token, *given)
        if first:
            columns = outs[-1]
        result.update(zip(steps, outs))
    return result


def lookups_kernel(scalars_ref, scenario_ref, direct_ref, evolve_ref, load_ref, *outs):
    shape = (SHARD, 128)
    diagonal = lax.broadcasted_iota(jnp.int32, shape, 0) == lax.broadcasted_iota(jnp.int32, shape, 1)

    def column(row):
        kept = jnp.where(diagonal, scalars_ref[row : row + 1, :], 0.0)
        return jnp.broadcast_to(jnp.sum(kept, axis=1, keepdims=True), shape)

    section = column(0).astype(jnp.int32)
    settings, sections = load_ref.shape
    scenario = scenario_ref[...]
    direct = evolve = plate = jnp.zeros(shape, jnp.float32)
    for k in range(sections):
        here = section == k
        load = jnp.zeros((1, 128), jnp.float32)
        for j in range(settings):
            load = jnp.where(scenario == j, load_ref[j, k], load)
        direct = jnp.where(here, direct_ref[k], direct)
        evolve = jnp.where(here, evolve_ref[k], evolve)
        plate = jnp.where(here, load, plate)
    for out_ref, value in zip(outs, (column(1), direct, evolve, plate)):
        out_ref[...] = value


def lookups(scalars, scenario_param, direct_table, evolve_table, load_table):
    on_chip = pl.BlockSpec(memory_space=pltpu.VMEM)
    scalar = pl.BlockSpec(memory_space=pltpu.SMEM)
    return pl.pallas_call(
        lookups_kernel,
        in_specs=[on_chip, on_chip, scalar, scalar, scalar],
        out_specs=[on_chip] * 4,
        out_shape=[jax.ShapeDtypeStruct((SHARD, 128), jnp.float32)] * 4,
        compiler_params=pltpu.CompilerParams(vmem_limit_bytes=16 * 1024 * 1024),
    )(scalars, scenario_param.reshape(1, 128), direct_table, evolve_table, load_table)


def summed_over_zl_and_x(partial):
    foreign, own = partial[0, 1], partial[0, 0]
    for dx in (2, 1, 3):
        foreign = foreign + rotated(partial[dx, 1], "x", dx)
    for dx in (2, 1, 3):
        own = own + rotated(partial[dx, 0], "x", dx)
    return own + rotated(foreign, "zl", 1)


def summed_over_zp(blocks):
    total = 0.0
    for p in (2, 1, 3, 0):
        total = total + moved(
            blocks[p * SHARD : (p + 1) * SHARD],
            lambda y, c, zp, zl, x: ((p + zp) % 4, zl, y, c, x),
        )
    return total


def local(
    kernel,
    self_stiffness,
    slip,
    state,
    stress,
    section_id,
    scenario_param,
    direct_table,
    evolve_table,
    load_table,
):
    place = jnp.stack([lax.axis_index(axis).astype(jnp.int32) for axis in AXES])
    kernel, place = lax.optimization_barrier((kernel, place))
    tile, token = split_tile(kernel)
    scalars = jnp.pad(
        jnp.stack([section_id.astype(jnp.float32), self_stiffness]), ((0, 6), (0, 128 - SHARD))
    )
    here = moved(jnp.concatenate([state, stress, scalars]), to_worker)
    here, token = lax.optimization_barrier((here, token))
    state_0 = here[:SHARD]
    stress_0 = here[SHARD : 2 * SHARD]
    stiffness, direct, evolve, plate = lookups(
        here[2 * SHARD :], scenario_param, direct_table, evolve_table, load_table
    )

    weights = (1.0, 2.0, 2.0, 1.0)
    offsets = (0.0, 0.5, 0.5, 1.0)
    sum_slip = sum_state = sum_stress = 0.0
    state_rate = stress_rate = None
    for phase in range(4):
        if phase == 0:
            state_now, stress_now = (state_0, stress_0)
        else:
            state_now = state_0 + offsets[phase] * step_size * state_rate
            stress_now = stress_0 + offsets[phase] * step_size * stress_rate
        slip_rate = jnp.exp((stress_now - evolve * state_now) / direct)
        mismatch = slip_rate - plate
        along_y = [mismatch] + [rotated(mismatch, "y", t) for t in (1, 2, 3)]
        own = jnp.concatenate(along_y)
        partial = product(place, tile, token, own, rotated(own, "core", 1), phase == 3)
        state_rate = jnp.exp(-state_now) - slip_rate
        sum_slip = sum_slip + weights[phase] * slip_rate
        sum_state = sum_state + weights[phase] * state_rate
        own_rate = -stiffness * mismatch
        blocks = summed_over_zl_and_x(partial)
        if phase == 3:
            break
        stress_rate = own_rate - summed_over_zp(blocks)
        sum_stress = sum_stress + weights[phase] * stress_rate
    back = moved(jnp.concatenate([sum_slip, sum_state, sum_stress + own_rate]), to_owner)
    coupled = blocks[:SHARD]
    for p in (2, 1, 3):
        coupled = coupled + rotated(blocks[p * SHARD : (p + 1) * SHARD], "zp", p)
    slip_new = slip + step_size / 6.0 * back[:SHARD]
    state_new = state + step_size / 6.0 * back[SHARD : 2 * SHARD]
    stress_new = stress + step_size / 6.0 * (back[2 * SHARD :] - coupled)
    return (slip_new, state_new, stress_new)


def solution(mesh):
    fine = Mesh(np.asarray(mesh.devices).reshape(SIZES), AXES)
    in_specs = (
        P(("y", "core"), ("zp", "zl", "x")),
        P(AXES),
        P(AXES, None),
        P(AXES, None),
        P(AXES, None),
        P(AXES),
        P(),
        P(),
        P(),
        P(),
    )
    out_specs = (P(AXES, None), P(AXES, None), P(AXES, None))
    return jax.shard_map(local, mesh=fine, in_specs=in_specs, out_specs=out_specs, check_vma=False)
```

```python
import jax
import jax.numpy as jnp
import numpy as np
from jax import lax
from jax.experimental import pallas as pl
from jax.experimental.pallas import tpu as pltpu
from jax.sharding import Mesh
from jax.sharding import PartitionSpec as P

step_size = 0.1
AXES = ("y", "core", "zp", "zl", "x")
SIZES = (4, 2, 4, 2, 4)
SHARD = 96
HALF = 4 * SHARD
SPREAD = (((2, 1),), ((1, 1), (3, 1)), ((0, 1), (2, 0), (1, 0), (3, 0), (0, 0)))


def index_of(place):
    index = 0
    for coordinate, size in zip(place, SIZES):
        index = index * size + coordinate
    return index


def moved(array, target):
    places = np.ndindex(*SIZES)
    return lax.ppermute(array, AXES, [(index_of(p), index_of(target(*p))) for p in places])


def rotated(array, axis, distance):
    size = SIZES[AXES.index(axis)]
    return lax.ppermute(array, axis, [(i, (i + distance) % size) for i in range(size)])


def to_worker(y, c, zp, zl, x):
    return (x, zl, y, c, zp)


def to_owner(y, c, zp, zl, x):
    return (zp, zl, x, c, y)


def split(value):
    high = value.astype(jnp.bfloat16)
    return high, (value - high.astype(jnp.float32)).astype(jnp.bfloat16)


def split_kernel(tile_ref, out_ref, token_ref):
    half = pl.program_id(0)
    token_ref[...] = jnp.zeros((8, 128), jnp.float32)
    high, low = split(tile_ref[...])
    out_ref[half // 2, half % 2, :, 0] = high.reshape(4, SHARD, 768)
    out_ref[half // 2, half % 2, :, 1] = low.reshape(4, SHARD, 768)


def split_tile(kernel):
    shape = (4, 2, 4, 2, SHARD, 768)
    return pl.pallas_call(
        split_kernel,
        grid=(8,),
        in_specs=[pl.BlockSpec((HALF, 768), lambda d: (d, 0))],
        out_specs=[pl.BlockSpec(memory_space=pltpu.VMEM), pl.BlockSpec((8, 128), lambda d: (0, 0))],
        out_shape=[pltpu.VMEM(shape, jnp.bfloat16), jax.ShapeDtypeStruct((8, 128), jnp.float32)],
        compiler_params=pltpu.CompilerParams(vmem_limit_bytes=20 * 1024 * 1024),
        cost_estimate=pl.CostEstimate(
            flops=4 * 3072 * 768, bytes_accessed=3072 * 768 * 8, transcendentals=0
        ),
    )(kernel)


def product_kernel(steps, last, first, *refs):
    place_ref, tile_ref, _, *refs = refs
    y, core, zp, zl, x = [place_ref[i] for i in range(5)]
    if first:
        own_ref, other_ref, columns_ref = refs[0], refs[1], refs[-1]
        outs = refs[2:-1]
        for half_ref, half in ((own_ref, core), (other_ref, 1 - core)):
            for t in range(4):
                high, low = split(half_ref[t * SHARD : (t + 1) * SHARD])
                start = half * HALF + lax.rem(y + 4 - t, 4) * SHARD
                rows = pl.ds(pl.multiple_of(start, SHARD), SHARD)
                columns_ref[rows, :128] = high
                columns_ref[rows, 128:] = low
    else:
        columns_ref, outs = refs[0], refs[1:]
    columns = columns_ref[...]
    for (dx, dz), out_ref in zip(steps, outs):
        there = lax.rem(x + dx, 4)
        half = lax.rem(zl + dz, 2)
        if last:
            tile = tile_ref[:, half, there]
        else:
            tile = tile_ref[there, half]
        sums = jnp.dot(
            tile.reshape(2 * HALF, 768), columns, preferred_element_type=jnp.float32
        ).reshape(4, 2, SHARD, 256)
        total = sums[:, 0, :, :128] + (sums[:, 0, :, 128:] + sums[:, 1, :, :128])
        for i in range(4):
            start = lax.rem(i + 4 - zp, 4) * SHARD
            out_ref[pl.ds(pl.multiple_of(start, SHARD), SHARD)] = total[i]


def product(place, tile, token, own, other, last):
    result = {}
    columns = None
    block = jax.ShapeDtypeStruct((HALF, 128), jnp.float32)
    on_chip = pl.BlockSpec(memory_space=pltpu.VMEM)
    for steps in SPREAD:
        first = columns is None
        given = (own, other) if first else (columns,)
        out_shape = [block] * len(steps)
        if first:
            out_shape.append(jax.ShapeDtypeStruct((768, 256), jnp.bfloat16))

        def body(*refs, steps=steps, first=first):
            product_kernel(steps, last, first, *refs)

        outs = pl.pallas_call(
            body,
            in_specs=[pl.BlockSpec(memory_space=pltpu.SMEM)] + [on_chip] * (2 + len(given)),
            out_specs=[on_chip] * len(out_shape),
            out_shape=out_shape,
            compiler_params=pltpu.CompilerParams(vmem_limit_bytes=16 * 1024 * 1024),
            cost_estimate=pl.CostEstimate(
                flops=len(steps) * 2 * 768 * 768 * 256, bytes_accessed=2 * 1024 * 1024, transcendentals=0
            ),
        )(place, tile, token, *given)
        if first:
            columns = outs[-1]
        result.update(zip(steps, outs))
    return result


def pack_kernel(state_ref, stress_ref, section_ref, stiffness_ref, out_ref):
    out_ref[:SHARD] = state_ref[...]
    out_ref[SHARD : 2 * SHARD] = stress_ref[...]
    out_ref[2 * SHARD :] = jnp.zeros((8, 128), jnp.float32)
    out_ref[2 * SHARD : 2 * SHARD + 1, :SHARD] = section_ref[...].astype(jnp.float32)
    out_ref[2 * SHARD + 1 : 2 * SHARD + 2, :SHARD] = stiffness_ref[...]


def packed(state, stress, section_id, self_stiffness):
    on_chip = pl.BlockSpec(memory_space=pltpu.VMEM)
    return pl.pallas_call(
        pack_kernel,
        in_specs=[on_chip] * 4,
        out_specs=on_chip,
        out_shape=jax.ShapeDtypeStruct((2 * SHARD + 8, 128), jnp.float32),
        compiler_params=pltpu.CompilerParams(vmem_limit_bytes=16 * 1024 * 1024),
    )(state, stress, section_id.reshape(1, SHARD), self_stiffness.reshape(1, SHARD))


def lookups_kernel(scalars_ref, scenario_ref, direct_ref, evolve_ref, load_ref, *outs):
    shape = (SHARD, 128)
    diagonal = lax.broadcasted_iota(jnp.int32, shape, 0) == lax.broadcasted_iota(jnp.int32, shape, 1)

    def column(row):
        kept = jnp.where(diagonal, scalars_ref[row : row + 1, :], 0.0)
        return jnp.broadcast_to(jnp.sum(kept, axis=1, keepdims=True), shape)

    section = column(0).astype(jnp.int32)
    settings, sections = load_ref.shape
    scenario = scenario_ref[...]
    direct = evolve = plate = jnp.zeros(shape, jnp.float32)
    for k in range(sections):
        here = section == k
        load = jnp.zeros((1, 128), jnp.float32)
        for j in range(settings):
            load = jnp.where(scenario == j, load_ref[j, k], load)
        direct = jnp.where(here, direct_ref[k], direct)
        evolve = jnp.where(here, evolve_ref[k], evolve)
        plate = jnp.where(here, load, plate)
    for out_ref, value in zip(outs, (column(1), direct, evolve, plate)):
        out_ref[...] = value


def lookups(scalars, scenario_param, direct_table, evolve_table, load_table):
    on_chip = pl.BlockSpec(memory_space=pltpu.VMEM)
    scalar = pl.BlockSpec(memory_space=pltpu.SMEM)
    return pl.pallas_call(
        lookups_kernel,
        in_specs=[on_chip, on_chip, scalar, scalar, scalar],
        out_specs=[on_chip] * 4,
        out_shape=[jax.ShapeDtypeStruct((SHARD, 128), jnp.float32)] * 4,
        compiler_params=pltpu.CompilerParams(vmem_limit_bytes=16 * 1024 * 1024),
    )(scalars, scenario_param.reshape(1, 128), direct_table, evolve_table, load_table)


def summed_over_zl_and_x(partial):
    foreign, own = partial[0, 1], partial[0, 0]
    for dx in (2, 1, 3):
        foreign = foreign + rotated(partial[dx, 1], "x", dx)
    for dx in (2, 1, 3):
        own = own + rotated(partial[dx, 0], "x", dx)
    return own + rotated(foreign, "zl", 1)


def summed_over_zp(blocks):
    total = 0.0
    for p in (2, 1, 3, 0):
        total = total + moved(
            blocks[p * SHARD : (p + 1) * SHARD],
            lambda y, c, zp, zl, x: ((p + zp) % 4, zl, y, c, x),
        )
    return total


def local(
    kernel,
    self_stiffness,
    slip,
    state,
    stress,
    section_id,
    scenario_param,
    direct_table,
    evolve_table,
    load_table,
):
    place = jnp.stack([lax.axis_index(axis).astype(jnp.int32) for axis in AXES])
    kernel, place = lax.optimization_barrier((kernel, place))
    tile, token = split_tile(kernel)
    here = moved(packed(state, stress, section_id, self_stiffness), to_worker)
    here, token = lax.optimization_barrier((here, token))
    state_0 = here[:SHARD]
    stress_0 = here[SHARD : 2 * SHARD]
    stiffness, direct, evolve, plate = lookups(
        here[2 * SHARD :], scenario_param, direct_table, evolve_table, load_table
    )

    weights = (1.0, 2.0, 2.0, 1.0)
    offsets = (0.0, 0.5, 0.5, 1.0)
    sum_slip = sum_state = sum_stress = 0.0
    state_rate = stress_rate = None
    for phase in range(4):
        if phase == 0:
            state_now, stress_now = (state_0, stress_0)
        else:
            state_now = state_0 + offsets[phase] * step_size * state_rate
            stress_now = stress_0 + offsets[phase] * step_size * stress_rate
        slip_rate = jnp.exp((stress_now - evolve * state_now) / direct)
        mismatch = slip_rate - plate
        along_y = [mismatch] + [rotated(mismatch, "y", t) for t in (1, 2, 3)]
        own = jnp.concatenate(along_y)
        partial = product(place, tile, token, own, rotated(own, "core", 1), phase == 3)
        state_rate = jnp.exp(-state_now) - slip_rate
        sum_slip = sum_slip + weights[phase] * slip_rate
        sum_state = sum_state + weights[phase] * state_rate
        own_rate = -stiffness * mismatch
        blocks = summed_over_zl_and_x(partial)
        if phase == 3:
            break
        stress_rate = own_rate - summed_over_zp(blocks)
        sum_stress = sum_stress + weights[phase] * stress_rate
    back = moved(jnp.concatenate([sum_slip, sum_state, sum_stress + own_rate]), to_owner)
    coupled = blocks[:SHARD]
    for p in (2, 1, 3):
        coupled = coupled + rotated(blocks[p * SHARD : (p + 1) * SHARD], "zp", p)
    slip_new = slip + step_size / 6.0 * back[:SHARD]
    state_new = state + step_size / 6.0 * back[SHARD : 2 * SHARD]
    stress_new = stress + step_size / 6.0 * (back[2 * SHARD :] - coupled)
    return (slip_new, state_new, stress_new)


def solution(mesh):
    fine = Mesh(np.asarray(mesh.devices).reshape(SIZES), AXES)
    in_specs = (
        P(("y", "core"), ("zp", "zl", "x")),
        P(AXES),
        P(AXES, None),
        P(AXES, None),
        P(AXES, None),
        P(AXES),
        P(),
        P(),
        P(),
        P(),
    )
    out_specs = (P(AXES, None), P(AXES, None), P(AXES, None))
    return jax.shard_map(local, mesh=fine, in_specs=in_specs, out_specs=out_specs, check_vma=False)
```
